32 devices in a mesh: seg: 2 (over y), row: 4 (over x, core), col: 4 (over z).
Axes of the slice: x: 2, y: 2, z: 4, core: 2. Of those that a mesh axis runs over, the one named last changes fastest.
Arguments:
- raw_traces: bfloat16 [8192, 16, 256], P(('seg', 'row', 'col')), parts along dimension 0, may hold values from -6 to 6
- channel_pick: int32 [4096], P(('seg', 'row', 'col')), parts along dimension 0, may hold values from 0 to 4095, as said below
- clip_mask: int32 [4096, 16], P(('seg', 'row', 'col')), parts along dimension 0, may hold values 0 or 1
Outputs:
- correlations: bfloat16 [4096, 2048, 128], P(('seg', 'row'), 'col'), parts along dimension 0
The draws below stay inside these ranges and needn't reach their ends.
There are 2 independent parts, one for each index of `seg`. The reference program is written for one: setup_inputs(seed, part) draws one part's arguments, and reference() takes and returns one part's arrays. A program takes and returns all parts, laid end to end along the dimension named above; each array names one. Nothing has to cross between parts.
Inputs may be any that keep to these rules, and one draw needn't show every extreme that they name: `channel_pick`: entry j is 2j or 2j+1; entry 0 is even and entry 2047 is odd.
All inputs are finite; a program needn't handle non-finite values. No bound on the sum of `clip_mask` on one device may be relied on, other than what follows from the above.
Results may differ from the reference program's by a relative error of at most 0.0057.
Values may be sent and summed in bfloat16 or wider, within the bound.
No kernel may reach another device: no remote copies, remote signals or barrier semaphores. Data moves between devices by JAX's collectives and lax.ppermute only.
A program may use at most 576 MiB of HBM per device.

```python
import math
import jax
import jax.numpy as jnp
from jax import lax

C = 2048
W = 16
S = 256
L = 128
K = 128
CR = 4096
TILE = 512
N_ROW = 4


def draw_channel_pick(key, part):
    bits = jax.random.randint(key, (C,), 0, 2, dtype=jnp.int32)
    position = jnp.arange(C, dtype=jnp.int32)
    bits = jnp.where(position == 0, 0, jnp.where(position == C - 1, 1, bits))
    return 2 * position + bits


def set_ends(drawn, key, smallest, largest):
    extent = drawn.shape
    place = [jax.random.randint(jax.random.fold_in(key, axis), (), 0, extent[axis]) for axis in range(len(extent))]
    drawn = drawn.at[tuple(place)].set(smallest)
    longest = extent.index(max(extent))
    place[longest] = (place[longest] + 1) % extent[longest]
    return drawn.at[tuple(place)].set(largest)


def steps_of(own_key, extent, split, low, high):
    gain, own = 1.0, jax.random.fold_in(own_key, 6)
    for dim, parts in split:
        steps = jnp.exp(jax.random.uniform(jax.random.fold_in(own, dim), (parts,), jnp.float32, low / len(split), high / len(split)))
        gain = gain * jnp.repeat(steps, extent[dim] // parts).reshape([-1 if axis == dim else 1 for axis in range(len(extent))])
    return gain


def scatter_about(key, shape, scale, reach, pieces=(), kind=jnp.bfloat16):
    result = jax.random.normal(key, shape, jnp.float32) * scale
    if len(pieces) > 0:
        result = steps_of(key, shape, pieces, -0.22, 0.18) * result
    return jnp.clip(result, min=-reach, max=reach).astype(kind)


def setup_inputs(seed: int = 0, part: int = 0) -> dict:
    key_list = jax.random.split(jax.random.key(seed), 4)
    part_keys = jax.random.split(jax.random.fold_in(key_list[3], part), 4)
    return {
        "raw_traces": scatter_about(part_keys[0], (CR, W, S), 1.0, 6.0, ((0, 16),)),
        "channel_pick": draw_channel_pick(jax.random.fold_in(jax.random.fold_in(key_list[3], part), 71), part),
        "clip_mask": set_ends((jax.random.randint(part_keys[2], (C, W), 0, 8) < 7).astype(jnp.int32), jax.random.fold_in(part_keys[2], 1), 0, 1),
    }


def whiten_block(picked, keep):
    samples = picked.shape[2]
    half = samples // 2
    pos = jnp.arange(samples, dtype=jnp.int32)
    freq = jnp.arange(1, half + 1, dtype=jnp.int32)
    phase = pos[:, None] * freq[None, :] % samples
    angle = phase.astype(jnp.float32) * (2.0 * math.pi / samples)
    table = jnp.concatenate([jnp.cos(angle), -jnp.sin(angle)], axis=1)
    flat = picked.astype(jnp.float32).reshape(-1, samples)
    spec = jnp.dot(flat, table, precision=lax.Precision.HIGHEST, preferred_element_type=jnp.float32)
    real_part = spec[:, :half]
    imag_part = spec[:, half:]
    power = real_part * real_part + imag_part * imag_part
    gap = jnp.abs(freq[:, None] - freq[None, :])
    band = jnp.where(gap <= 2, 0.2, 0.0).astype(jnp.float32)
    smooth = jnp.dot(power, band, precision=lax.Precision.HIGHEST, preferred_element_type=jnp.float32)
    denom = jnp.sqrt(smooth + 0.1 * lax.optimization_barrier(jnp.mean(power, axis=1, keepdims=True)) + 1e-06)
    weight = keep.reshape(-1, 1).astype(jnp.float32) / denom
    whitened = jnp.concatenate([real_part * weight, imag_part * weight], axis=1)
    return whitened.astype(jnp.bfloat16).reshape(picked.shape[0], picked.shape[1], samples)

def lag_tables(half, samples, lags, windows):
    freq = jnp.arange(1, half + 1, dtype=jnp.int32)
    shift = jnp.arange(lags, dtype=jnp.int32) - lags // 2
    phase = freq[:, None] * shift[None, :] % samples
    angle = phase.astype(jnp.float32) * (2.0 * math.pi / samples)
    scale = 1.0 / math.sqrt(windows * half)
    return (jnp.cos(angle) * scale, jnp.sin(angle) * scale)

def reference(raw_traces, channel_pick, clip_mask):
    picked = raw_traces[channel_pick]
    spectra = whiten_block(picked, clip_mask)
    stacked = spectra.astype(jnp.float32).reshape(C, W, 2, K)
    rotated = jnp.concatenate([-spectra[:, :, K:], spectra[:, :, :K]], axis=2).astype(jnp.float32).reshape(C, W, 2, K)
    cos_table, sin_table = lag_tables(K, S, L, W)
    columns = jnp.arange(C, dtype=jnp.int32)

    def one_block(start):
        rows = lax.dynamic_slice_in_dim(stacked, start, TILE, 0)
        cross_re = jnp.einsum('iwpk,jwpk->ijk', rows, stacked, precision=lax.Precision.HIGHEST)
        cross_im = jnp.einsum('iwpk,jwpk->ijk', rows, rotated, precision=lax.Precision.HIGHEST)
        lagged = jnp.dot(cross_re.reshape(-1, K), cos_table, precision=lax.Precision.HIGHEST, preferred_element_type=jnp.float32)
        lagged = lagged - jnp.dot(cross_im.reshape(-1, K), sin_table, precision=lax.Precision.HIGHEST, preferred_element_type=jnp.float32)
        lagged = lagged.reshape(TILE, C, L)
        row_ids = start + jnp.arange(TILE, dtype=jnp.int32)
        same = row_ids[:, None] == columns[None, :]
        return jnp.where(same[:, :, None], 0.0, lagged).astype(jnp.bfloat16)
    starts = jnp.arange(N_ROW, dtype=jnp.int32) * TILE
    blocks = lax.map(one_block, starts)
    return blocks.reshape(C, C, L)
```

```python
import functools
import math

import jax
import jax.numpy as jnp
import ml_dtypes
import numpy as np
from jax import lax
from jax.experimental import pallas as pl
from jax.experimental.pallas import tpu as pltpu
from jax.sharding import PartitionSpec as P

L = 128
LANES = 128
PAD = 8


def spectrum_tables(samples):
    half = samples // 2
    freq = np.arange(1, half + 1)
    pos = np.arange(samples)
    angle = (freq[:, None] * pos[None, :] % samples) * (2.0 * np.pi / samples)
    table = np.concatenate([np.cos(angle), -np.sin(angle)], axis=0).astype(np.float32)
    high = table.astype(ml_dtypes.bfloat16)
    low = (table - high.astype(np.float32)).astype(ml_dtypes.bfloat16)
    return high, low


def lag_table(samples, lags, windows):
    half = samples // 2
    freq = np.arange(1, half + 1)
    shift = np.arange(lags) - lags // 2
    angle = (freq[:, None] * shift[None, :] % samples) * (2.0 * np.pi / samples)
    scale = 1.0 / math.sqrt(windows * half)
    table = np.concatenate([np.cos(angle), -np.sin(angle)], axis=0) * scale
    return table.astype(ml_dtypes.bfloat16)


def whiten_kernel(raw_ref, keep_ref, high_ref, low_ref, z_ref, rows_ref):
    windows = raw_ref.shape[0]
    half = high_ref.shape[0] // 2
    parts = 2 * windows
    pitch = parts + PAD
    contract = (((1,), (1,)), ((), ()))

    def window(w, carry):
        raw = raw_ref[w]
        spec = lax.dot_general(high_ref[...], raw, contract, preferred_element_type=jnp.float32)
        spec += lax.dot_general(low_ref[...], raw, contract, preferred_element_type=jnp.float32)
        real, imag = spec[:half], spec[half:]
        power = real * real + imag * imag
        total = power
        for gap in (1, 2):
            edge = jnp.zeros((gap, power.shape[1]), jnp.float32)
            total += jnp.concatenate([power[gap:], edge], axis=0)
            total += jnp.concatenate([edge, power[:-gap]], axis=0)
        mean = jnp.sum(power, axis=0, keepdims=True) * (1.0 / half)
        denom = jnp.sqrt(total * 0.2 + 0.1 * mean + 1e-06)
        weight = keep_ref[pl.ds(w, 1), :] / denom
        rows_ref[pl.ds(w, half, stride=pitch), :] = real * weight
        rows_ref[pl.ds(windows + w, half, stride=pitch), :] = imag * weight
        return carry

    lax.fori_loop(0, windows, window, 0, unroll=4)

    def narrow(k, carry):
        start = pl.multiple_of(k * pitch, 8)
        z_ref[k] = rows_ref[pl.ds(start, parts), :].astype(jnp.bfloat16)
        return carry

    lax.fori_loop(0, half, narrow, 0, unroll=8)


def whiten(picked, keep):
    windows, channels, samples = picked.shape
    half = samples // 2
    high, low = spectrum_tables(samples)
    return pl.pallas_call(
        whiten_kernel,
        grid=(channels // LANES,),
        in_specs=[
            pl.BlockSpec((windows, LANES, samples), lambda c: (0, c, 0)),
            pl.BlockSpec((windows, LANES), lambda c: (0, c)),
            pl.BlockSpec((samples, samples), lambda c: (0, 0)),
            pl.BlockSpec((samples, samples), lambda c: (0, 0)),
        ],
        out_specs=pl.BlockSpec((half, 2 * windows, LANES), lambda c: (0, 0, c)),
        out_shape=jax.ShapeDtypeStruct((half, 2 * windows, channels), jnp.bfloat16),
        scratch_shapes=[pltpu.VMEM((half * (2 * windows + PAD), LANES), jnp.float32)],
        compiler_params=pltpu.CompilerParams(vmem_limit_bytes=32 * 2**20),
        name="whiten",
    )(picked, keep, jnp.asarray(high), jnp.asarray(low))


def pairs_kernel(place_ref, a_ref, b_ref, t_ref, *rest, nk, steps):
    o_ref, even_ref, odd_ref = rest[-3:]
    g = pl.program_id(0)
    half = a_ref.shape[1]
    windows = a_ref.shape[2] // 2
    chans = o_ref.shape[0]
    pitch = 2 * half + PAD
    rounds = half // nk
    ni = chans // rounds

    def cross(x_ref, it):
        for u in range(nk):
            k = it * nk + u
            a = a_ref[0, k]
            b = b_ref[0, k]
            turned = jnp.concatenate([-b[windows:], b[:windows]], axis=0)
            both = jnp.concatenate([b, turned], axis=1)
            y = lax.dot_general(
                a, both, (((0,), (0,)), ((), ())), preferred_element_type=jnp.float32
            )
            x_ref[pl.ds(k, chans, stride=pitch), :] = y[:, :LANES]
            x_ref[pl.ds(half + k, chans, stride=pitch), :] = y[:, LANES:]

    def lag(x_ref, it):
        for u in range(ni):
            i = it * ni + u
            start = pl.multiple_of(i * pitch, 8)
            x = x_ref[pl.ds(start, 2 * half), :].astype(jnp.bfloat16)
            y = lax.dot_general(
                x, t_ref[...], (((0,), (0,)), ((), ())), preferred_element_type=jnp.float32
            )
            o_ref[i] = y.astype(jnp.bfloat16)

    def loop(body):
        lax.fori_loop(0, rounds, lambda it, carry: (body(it), carry)[1], 0)

    def both_of(new_ref, old_ref):
        def body(it):
            lag(old_ref, it)
            cross(new_ref, it)

        loop(body)

    last = steps
    pl.when(g == 0)(lambda: loop(lambda it: cross(even_ref, it)))
    if steps > 1:
        middle = (g > 0) & (g < last)
        pl.when(middle & (g % 2 == 0))(lambda: both_of(even_ref, odd_ref))
        pl.when(middle & (g % 2 == 1))(lambda: both_of(odd_ref, even_ref))
    tail_ref = odd_ref if last % 2 == 0 else even_ref
    pl.when(g == last)(lambda: loop(lambda it: lag(tail_ref, it)))

    back = jnp.maximum(g - 1, 0)

    @pl.when((g > 0) & (place_ref[4 * back + 2] == place_ref[4 * back + 3]))
    def _():
        def clear(i, carry):
            start = pl.multiple_of(i // 16 * 16, 16)
            rows = o_ref[i, pl.ds(start, 16), :]
            ids = lax.broadcasted_iota(jnp.int32, rows.shape, 0) + start
            o_ref[i, pl.ds(start, 16), :] = jnp.where(ids == i, 0.0, rows.astype(jnp.float32)).astype(
                jnp.bfloat16
            )
            return carry

        lax.fori_loop(0, chans, clear, 0, unroll=8)


def correlate(rows, cols, table, place, shape, out):
    half = rows.shape[1]
    parts = rows.shape[2]
    table_spec = pl.BlockSpec(table.shape, lambda g, p: (0, 0))
    slots, blocks, steps = place

    def now(g):
        return jnp.minimum(g, steps - 1)

    def before(g):
        return jnp.maximum(g - 1, 0)

    nrow, ncol = shape[0] // LANES, shape[1] // LANES
    inputs = [rows, cols, table]
    in_specs = [
        pl.BlockSpec((1, half, parts, LANES), lambda g, p: (slots[0](now(g)), 0, 0, 0)),
        pl.BlockSpec((1, half, parts, LANES), lambda g, p: (slots[1](now(g)), 0, 0, 0)),
        table_spec,
    ]
    aliases = {}
    if out is not None:
        inputs.append(out)
        in_specs.append(pl.BlockSpec(memory_space=pl.ANY))
        aliases = {4: 0}
    return pl.pallas_call(
        functools.partial(pairs_kernel, nk=min(32, half), steps=steps),
        grid_spec=pltpu.PrefetchScalarGridSpec(
            num_scalar_prefetch=1,
            grid=(steps + 1,),
            in_specs=in_specs,
            out_specs=pl.BlockSpec(
                (LANES, LANES, shape[2]),
                lambda g, p: (p[4 * before(g)], p[4 * before(g) + 1], 0),
            ),
            scratch_shapes=[pltpu.VMEM((LANES * (2 * half + PAD), LANES), jnp.float32)] * 2,
        ),
        out_shape=jax.ShapeDtypeStruct(shape, jnp.bfloat16),
        input_output_aliases=aliases,
        compiler_params=pltpu.CompilerParams(vmem_limit_bytes=56 * 2**20),
        cost_estimate=pl.CostEstimate(
            flops=int((7 * steps + 5) * 1e9), bytes_accessed=steps * 2**22, transcendentals=0
        ),
        name="pairs",
    )(blocks, *inputs)


def rectangle(nr, nc, first_row, first_col, here, row, col, turn_r, turn_c):
    slots = (lambda g: g // nc, lambda g: g % nc)
    step = jnp.arange(nr * nc, dtype=jnp.int32)
    row_block = (here + first_row + step // nc) % turn_r
    col_block = (here + first_col + step % nc) % turn_c
    blocks = jnp.stack(
        [row_block, col_block, row * turn_r + row_block, col * turn_c + col_block], axis=1
    ).reshape(-1)
    return slots, blocks, nr * nc


def local(raw_traces, channel_pick, clip_mask, *, n_row, n_col):
    owned = channel_pick.shape[0]
    windows = raw_traces.shape[1]
    samples = raw_traces.shape[2]
    half = samples // 2
    row, col = lax.axis_index("row"), lax.axis_index("col")
    paired = raw_traces.reshape(owned, 2, windows, samples)
    parity = (channel_pick % 2)[:, None, None]
    picked = jnp.where(parity == 1, paired[:, 1], paired[:, 0]).transpose(1, 0, 2)
    keep = clip_mask.astype(jnp.float32).T
    table = jnp.asarray(lag_table(samples, L, windows))
    tile_r, tile_c = owned * n_col, owned * n_row
    shape = (tile_r, tile_c, L)

    if owned % LANES != 0 or n_row != n_col or n_row % 2 or n_row & (n_row - 1):
        fill = -owned % LANES
        picked = jnp.pad(picked, ((0, 0), (0, fill), (0, 0)))
        keep = jnp.pad(keep, ((0, 0), (0, fill)))
        z = whiten(picked, keep)[:, :, :owned]
        first = lax.all_gather(z, "col", axis=2, tiled=True)
        mine = jnp.where(row == col, first, 0).astype(first.dtype)
        second = lax.psum(mine, "row")

        def blocked(v):
            return v.reshape(half, 2 * windows, -1, LANES).transpose(2, 0, 1, 3)

        nr, nc = tile_r // LANES, tile_c // LANES
        place = rectangle(nr, nc, 0, 0, 0, row, col, nr, nc)
        return correlate(blocked(first), blocked(second), table, place, shape, None)

    z = whiten(picked, keep)
    n = n_col
    ring = [(j, (j - 1) % n) for j in range(n)]
    per = owned // LANES

    def share(v):
        held = {c: {c} for c in range(n_col)}
        bit = n_row // 2
        while bit:
            moves = [(r * n_col + c, (r ^ bit) * n_col + c) for c in range(n_col) for r in sorted(held[c])]
            got = lax.ppermute(v, ("row", "col"), moves)
            mask = ~(2 * bit - 1)
            keeps = ((row ^ col) & bit) == 0
            v = jnp.where(keeps, v, got)
            for c in range(n_col):
                held[c] |= {r ^ bit for r in held[c]}
            bit //= 2
        return v

    def split(v):
        return v.reshape(half, 2 * windows, per, LANES).transpose(2, 0, 1, 3)

    rows = [split(z)]
    for _ in range(n - 1):
        rows.append(lax.ppermute(rows[-1], "col", ring))
    cols = [share(v) for v in rows]
    out = None
    chunk = 2
    row_groups = [jnp.concatenate(rows[s : s + chunk]) for s in range(0, n, chunk)]
    col_groups = [jnp.concatenate(cols[s : s + chunk]) for s in range(0, n, chunk)]
    for late in range(len(row_groups)):
        for r, c in [(late, q) for q in range(late)] + [(q, late) for q in range(late + 1)]:
            place = rectangle(
                chunk * per, chunk * per, r * chunk * per, c * chunk * per, col * per, row, col, n * per, n * per
            )
            out = correlate(row_groups[r], col_groups[c], table, place, shape, out)
    return out


def solution(mesh):
    return jax.shard_map(
        functools.partial(local, n_row=mesh.shape["row"], n_col=mesh.shape["col"]),
        mesh=mesh,
        in_specs=(
            P(("seg", "row", "col"), None, None),
            P(("seg", "row", "col")),
            P(("seg", "row", "col"), None),
        ),
        out_specs=P(("seg", "row"), "col", None),
        check_vma=False,
    )
```

```python
import functools
import math

import jax
import jax.numpy as jnp
import ml_dtypes
import numpy as np
from jax import lax
from jax.experimental import pallas as pl
from jax.experimental.pallas import tpu as pltpu
from jax.sharding import PartitionSpec as P

L = 128
LANES = 128
PAD = 8


def spectrum_tables(samples):
    half = samples // 2
    freq = np.arange(1, half + 1)
    pos = np.arange(samples)
    angle = (freq[:, None] * pos[None, :] % samples) * (2.0 * np.pi / samples)
    table = np.concatenate([np.cos(angle), -np.sin(angle)], axis=0).astype(np.float32)
    high = table.astype(ml_dtypes.bfloat16)
    low = (table - high.astype(np.float32)).astype(ml_dtypes.bfloat16)
    return np.stack([high, low])


def lag_table(samples, lags, windows):
    half = samples // 2
    freq = np.arange(1, half + 1)
    shift = np.arange(lags) - lags // 2
    angle = (freq[:, None] * shift[None, :] % samples) * (2.0 * np.pi / samples)
    scale = 1.0 / math.sqrt(windows * half)
    table = np.concatenate([np.cos(angle), -np.sin(angle)], axis=0) * scale
    return table.T.astype(ml_dtypes.bfloat16)


def whiten_kernel(raw_ref, keep_ref, table_ref, z_ref, rows_ref):
    windows = raw_ref.shape[0]
    half = table_ref.shape[1] // 2
    parts = 2 * windows
    pitch = parts + PAD
    contract = (((1,), (1,)), ((), ()))

    def window(w, carry):
        raw = raw_ref[w]
        spec = lax.dot_general(table_ref[0], raw, contract, preferred_element_type=jnp.float32)
        spec += lax.dot_general(table_ref[1], raw, contract, preferred_element_type=jnp.float32)
        real, imag = spec[:half], spec[half:]
        power = real * real + imag * imag
        total = power
        for gap in (1, 2):
            edge = jnp.zeros((gap, power.shape[1]), jnp.float32)
            total += jnp.concatenate([power[gap:], edge], axis=0)
            total += jnp.concatenate([edge, power[:-gap]], axis=0)
        mean = jnp.sum(power, axis=0, keepdims=True) * (1.0 / half)
        denom = jnp.sqrt(total * 0.2 + 0.1 * mean + 1e-06)
        weight = keep_ref[pl.ds(w, 1), :] / denom
        rows_ref[pl.ds(w, half, stride=pitch), :] = real * weight
        rows_ref[pl.ds(windows + w, half, stride=pitch), :] = imag * weight
        return carry

    lax.fori_loop(0, windows, window, 0, unroll=4)

    def narrow(k, carry):
        start = pl.multiple_of(k * pitch, 8)
        z_ref[k] = rows_ref[pl.ds(start, parts), :].astype(jnp.bfloat16)
        return carry

    lax.fori_loop(0, half, narrow, 0, unroll=8)


def whiten(picked, keep):
    windows, channels, samples = picked.shape
    half = samples // 2
    return pl.pallas_call(
        whiten_kernel,
        grid=(channels // LANES,),
        in_specs=[
            pl.BlockSpec((windows, LANES, samples), lambda c: (0, c, 0)),
            pl.BlockSpec((windows, LANES), lambda c: (0, c)),
            pl.BlockSpec((2, samples, samples), lambda c: (0, 0, 0)),
        ],
        out_specs=pl.BlockSpec((half, 2 * windows, LANES), lambda c: (0, 0, c)),
        out_shape=jax.ShapeDtypeStruct((half, 2 * windows, channels), jnp.bfloat16),
        scratch_shapes=[pltpu.VMEM((half * (2 * windows + PAD), LANES), jnp.float32)],
        compiler_params=pltpu.CompilerParams(vmem_limit_bytes=32 * 2**20),
        name="whiten",
    )(picked, keep, jnp.asarray(spectrum_tables(samples)))


def pairs_kernel(slots_ref, here_ref, *refs, pairs, nr, routes, nk, turn):
    rows, cols = refs[:nr], []
    at = nr
    for route in routes:
        cols.append(list(zip(refs[at : at + len(route)], route, strict=True)))
        at += len(route)
    t_ref = refs[at]
    o_ref, even_ref, odd_ref, a_ref, b_ref, a_sem, b_sem = refs[-7:]
    g = pl.program_id(0)
    last = len(pairs)
    half = a_ref.shape[1]
    windows = a_ref.shape[2] // 2
    chans = o_ref.shape[0]
    pitch = 2 * half + PAD
    rounds = half // nk
    ni = chans // rounds

    def row_copy(step):
        slot = step % 2
        return pltpu.make_async_copy(rows[pairs[step][0]], a_ref.at[slot], a_sem.at[slot])

    def col_copy(step, ref):
        slot = step % 2
        return pltpu.make_async_copy(ref, b_ref.at[slot], b_sem.at[slot])

    def start(step):
        row_copy(step).start()
        for ref, ways in cols[pairs[step][1]]:
            here = functools.reduce(jnp.logical_or, [here_ref[3] == way for way in ways])
            pl.when(here)(lambda: col_copy(step, ref).start())

    pl.when(g == 0)(lambda: start(0))
    for step in range(last):

        @pl.when(g == step)
        def _():
            if step + 1 < last:
                start(step + 1)
            row_copy(step).wait()
            col_copy(step, cols[pairs[step][1]][0][0]).wait()

    def cross(x_ref, it, slot):
        for u in range(nk):
            k = it * nk + u
            a = a_ref[slot, k]
            b = b_ref[slot, k]
            turned = jnp.concatenate([-b[windows:], b[:windows]], axis=0)
            both = jnp.concatenate([b, turned], axis=1)
            y = lax.dot_general(
                a, both, (((0,), (0,)), ((), ())), preferred_element_type=jnp.float32
            )
            x_ref[pl.ds(k, chans, stride=pitch), :] = y[:, :LANES]
            x_ref[pl.ds(half + k, chans, stride=pitch), :] = y[:, LANES:]

    def slab(x_ref, i):
        start = pl.multiple_of(i * pitch, 8)
        return x_ref[pl.ds(start, 2 * half), :].astype(jnp.bfloat16)

    def lag(x_ref, it):
        for u in range(0, ni, 2):
            i = it * ni + u
            x = jnp.concatenate([slab(x_ref, i), slab(x_ref, i + 1)], axis=1)
            y = jnp.dot(t_ref[...], x, preferred_element_type=jnp.float32).astype(jnp.bfloat16)
            o_ref[i] = y[:, :LANES].T
            o_ref[i + 1] = y[:, LANES:].T

    def loop(body):
        lax.fori_loop(0, rounds, lambda it, carry: (body(it), carry)[1], 0)

    def both_of(new_ref, old_ref, slot):
        def body(it):
            lag(old_ref, it)
            cross(new_ref, it, slot)

        loop(body)

    pl.when(g == 0)(lambda: loop(lambda it: cross(even_ref, it, 0)))
    if last > 1:
        middle = (g > 0) & (g < last)
        pl.when(middle & (g % 2 == 1))(lambda: both_of(odd_ref, even_ref, 1))
    if last > 2:
        pl.when(middle & (g % 2 == 0))(lambda: both_of(even_ref, odd_ref, 0))
    tail_ref = odd_ref if last % 2 == 0 else even_ref
    pl.when(g == last)(lambda: loop(lambda it: lag(tail_ref, it)))

    back = jnp.maximum(g - 1, 0)

    block_r, block_c = block_at(back, slots_ref, here_ref, turn)
    first_r, first_c = here_ref[0] * turn[0], here_ref[1] * turn[1]

    @pl.when((g > 0) & (first_r + block_r == first_c + block_c))
    def _():
        def clear(i, carry):
            start = pl.multiple_of(i // 16 * 16, 16)
            rows = o_ref[i, pl.ds(start, 16), :]
            ids = lax.broadcasted_iota(jnp.int32, rows.shape, 0) + start
            kept = jnp.where(ids == i, 0.0, rows.astype(jnp.float32))
            o_ref[i, pl.ds(start, 16), :] = kept.astype(jnp.bfloat16)
            return carry

        lax.fori_loop(0, chans, clear, 0, unroll=8)


def block_at(step, slots_ref, here_ref, turn):
    block_r = lax.rem(slots_ref[2 * step] + here_ref[2], turn[0])
    block_c = lax.rem(slots_ref[2 * step + 1] + here_ref[2], turn[1])
    return block_r, block_c


def correlate(rows, cols, pairs, table, here, shape, out):
    half, parts = rows[0].shape[:2]
    turn = (shape[0] // LANES, shape[1] // LANES)
    slots = jnp.asarray(np.array(pairs, np.int32).reshape(-1))

    def before(g):
        return jnp.maximum(g - 1, 0)

    used_r, used_c = sorted({r for r, _ in pairs}), sorted({c for _, c in pairs})
    pairs = [(used_r.index(r), used_c.index(c)) for r, c in pairs]
    whole = pl.BlockSpec(memory_space=pl.ANY)
    inputs = [rows[r] for r in used_r] + [v for c in used_c for v, _ in cols[c]]
    routes = [[ways for _, ways in cols[c]] for c in used_c]
    in_specs = [whole] * len(inputs) + [pl.BlockSpec(table.shape, lambda g, p, q: (0, 0))]
    inputs.append(table)
    aliases = {}
    if out is not None:
        aliases = {len(inputs) + 2: 0}
        inputs.append(out)
        in_specs.append(whole)
    steps = len(pairs)
    buffer = pltpu.VMEM((2, half, parts, LANES), jnp.bfloat16)
    return pl.pallas_call(
        functools.partial(
            pairs_kernel, pairs=pairs, nr=len(used_r), routes=routes, nk=half, turn=turn
        ),
        grid_spec=pltpu.PrefetchScalarGridSpec(
            num_scalar_prefetch=2,
            grid=(steps + 1,),
            in_specs=in_specs,
            out_specs=pl.BlockSpec(
                (LANES, LANES, shape[2]),
                lambda g, p, q: (*block_at(before(g), p, q, turn), 0),
            ),
            scratch_shapes=[pltpu.VMEM((LANES * (2 * half + PAD), LANES), jnp.float32)] * 2
            + [buffer, buffer, pltpu.SemaphoreType.DMA((2,)), pltpu.SemaphoreType.DMA((2,))],
        ),
        out_shape=jax.ShapeDtypeStruct(shape, jnp.bfloat16),
        input_output_aliases=aliases,
        compiler_params=pltpu.CompilerParams(vmem_limit_bytes=56 * 2**20),
        cost_estimate=pl.CostEstimate(
            flops=int((7 * steps + 5) * 1e9), bytes_accessed=steps * 2**22, transcendentals=0
        ),
        name="pairs",
    )(slots, here, *inputs)


def hop(v, bit, held, n_col):
    moves = [(r * n_col + c, (r ^ bit) * n_col + c) for c in range(n_col) for r in sorted(held[c])]
    for kept in held:
        kept |= {r ^ bit for r in kept}
    return lax.ppermute(v, ("row", "col"), moves)


def send(v, n_row, n_col):
    return [
        lax.ppermute(v, ("row", "col"), [(c * n_col + c, (c ^ d) * n_col + c) for c in range(n_col)])
        for d in range(1, n_row)
    ]


def gate(v, after):
    return lax.optimization_barrier((v, after))[0]


def local(raw_traces, channel_pick, clip_mask, *, n_row, n_col):
    owned = channel_pick.shape[0]
    windows = raw_traces.shape[1]
    samples = raw_traces.shape[2]
    half = samples // 2
    row, col = lax.axis_index("row"), lax.axis_index("col")
    paired = raw_traces.reshape(owned, 2, windows, samples)
    parity = (channel_pick % 2)[:, None, None]
    picked = jnp.where(parity == 1, paired[:, 1], paired[:, 0]).transpose(1, 0, 2)
    keep = clip_mask.astype(jnp.float32).T
    table = jnp.asarray(lag_table(samples, L, windows))
    tile_r, tile_c = owned * n_col, owned * n_row
    shape = (tile_r, tile_c, L)

    if owned != LANES or n_row != n_col or n_row & (n_row - 1) or n_row < 4:
        fill = -owned % LANES
        picked = jnp.pad(picked, ((0, 0), (0, fill), (0, 0)))
        keep = jnp.pad(keep, ((0, 0), (0, fill)))
        z = whiten(picked, keep)[:, :, :owned]
        first = lax.all_gather(z, "col", axis=2, tiled=True)
        second = lax.psum(jnp.where(row == col, first, 0).astype(first.dtype), "row")
        nr, nc = tile_r // LANES, tile_c // LANES
        rows = jnp.split(first, nr, axis=2)
        cols = [[(v, [0])] for v in jnp.split(second, nc, axis=2)]
        pairs = [(r, c) for r in range(nr) for c in range(nc)]
        return correlate(rows, cols, pairs, table, jnp.stack([row, col, 0 * col, 0 * col]), shape, None)

    n = n_col
    ring = [(j, (j - 1) % n) for j in range(n)]
    here = jnp.stack([row, col, col, row ^ col])

    def step(pairs, out):
        return correlate(rows, cols, pairs, table, here, shape, out)

    def spread(v, got, held):
        bit = n_row // 2
        while bit > 1:
            v = jnp.where(((row ^ col) & bit) == 0, v, got)
            bit //= 2
            got = hop(v, bit, held, n_col)
        return [(v, list(range(0, n_row, 2))), (got, list(range(1, n_row, 2)))]

    def only(v):
        return jnp.where(row == col, v, 0).astype(v.dtype)

    top = n_row // 2
    rows = [whiten(picked, keep)]
    rows.append(lax.ppermute(rows[0], "col", ring))
    held = [{c} for c in range(n_col)]
    cols = [spread(rows[0], hop(only(rows[0]), top, held, n_col), held)]
    out = None
    pairs = [(0, 0), (1, 0)]
    for s in range(2, n + 1):
        if s < n:
            rows.append(lax.ppermute(rows[s - 1], "col", ring))
        if s == 2:
            held = [{c} for c in range(n_col)]
            coming = [hop(only(rows[1]), top, held, n_col)]
        else:
            coming = send(only(rows[s - 1]), n_row, n_col)
        out = step(pairs, out)
        if s < n:
            rows[s] = gate(rows[s], out)
        coming = [gate(v, out) for v in coming]
        if s == 2:
            cols.append(spread(rows[1], coming[0], held))
        else:
            cols.append([(v, [d]) for d, v in enumerate([rows[s - 1], *coming])])
        pairs = [(r, s - 1) for r in range(min(s, n - 1) + 1)] + [(s, c) for c in range(s - 1) if s < n]
    return step(pairs, out)


def solution(mesh):
    return jax.shard_map(
        functools.partial(local, n_row=mesh.shape["row"], n_col=mesh.shape["col"]),
        mesh=mesh,
        in_specs=(
            P(("seg", "row", "col"), None, None),
            P(("seg", "row", "col")),
            P(("seg", "row", "col"), None),
        ),
        out_specs=P(("seg", "row"), "col", None),
        check_vma=False,
    )
```

```python
import functools
import math

import jax
import jax.numpy as jnp
import ml_dtypes
import numpy as np
from jax import lax
from jax.experimental import pallas as pl
from jax.experimental.pallas import tpu as pltpu
from jax.sharding import PartitionSpec as P

L = 128
LANES = 128
PAD = 8
TAIL = 4


def spectrum_tables(samples):
    half = samples // 2
    freq = np.arange(1, half + 1)
    pos = np.arange(samples)
    angle = (freq[:, None] * pos[None, :] % samples) * (2.0 * np.pi / samples)
    table = np.concatenate([np.cos(angle), -np.sin(angle)], axis=0).astype(np.float32)
    high = table.astype(ml_dtypes.bfloat16)
    low = (table - high.astype(np.float32)).astype(ml_dtypes.bfloat16)
    return np.stack([high, low])


def lag_table(samples, lags, windows):
    half = samples // 2
    freq = np.arange(1, half + 1)
    shift = np.arange(lags) - lags // 2
    angle = (freq[:, None] * shift[None, :] % samples) * (2.0 * np.pi / samples)
    scale = 1.0 / math.sqrt(windows * half)
    table = np.concatenate([np.cos(angle), -np.sin(angle)], axis=0) * scale
    return table.T.astype(ml_dtypes.bfloat16)


def whiten_kernel(pick_ref, raw_ref, clip_ref, table_ref, z_ref, rows_ref, keep_ref, *picked):
    windows = raw_ref.shape[2]
    gap = windows + PAD
    first = pl.program_id(0) * LANES
    half = table_ref.shape[1] // 2
    parts = 2 * windows
    pitch = parts + PAD
    contract = (((1,), (1,)), ((), ()))
    keep_ref[...] = clip_ref[...].astype(jnp.float32).T

    def pull(j, carry):
        record = raw_ref[j, lax.rem(pick_ref[first + j], 2)].astype(jnp.float32)
        start = pl.multiple_of(j * gap, 8)
        for q, part in enumerate(picked):
            part[pl.ds(start, windows), :] = record[:, q * LANES : (q + 1) * LANES]
        return carry

    lax.fori_loop(0, LANES, pull, 0, unroll=8)

    def window(w, carry):
        raw = jnp.concatenate([part[pl.ds(w, LANES, stride=gap), :] for part in picked], axis=1)
        raw = raw.astype(jnp.bfloat16)
        spec = lax.dot_general(table_ref[0], raw, contract, preferred_element_type=jnp.float32)
        spec += lax.dot_general(table_ref[1], raw, contract, preferred_element_type=jnp.float32)
        real, imag = spec[:half], spec[half:]
        power = real * real + imag * imag
        total = power
        for far in (1, 2):
            edge = jnp.zeros((far, power.shape[1]), jnp.float32)
            total += jnp.concatenate([power[far:], edge], axis=0)
            total += jnp.concatenate([edge, power[:-far]], axis=0)
        mean = jnp.sum(power, axis=0, keepdims=True) * (1.0 / half)
        denom = jnp.sqrt(total * 0.2 + 0.1 * mean + 1e-06)
        weight = keep_ref[pl.ds(w, 1), :] / denom
        rows_ref[pl.ds(w, half, stride=pitch), :] = real * weight
        rows_ref[pl.ds(windows + w, half, stride=pitch), :] = imag * weight
        return carry

    lax.fori_loop(0, windows, window, 0, unroll=4)

    def narrow(k, carry):
        start = pl.multiple_of(k * pitch, 8)
        z_ref[k] = rows_ref[pl.ds(start, parts), :].astype(jnp.bfloat16)
        return carry

    lax.fori_loop(0, half, narrow, 0, unroll=8)


def whiten(raw, pick, clip):
    channels, _, windows, samples = raw.shape
    half = samples // 2
    return pl.pallas_call(
        whiten_kernel,
        grid_spec=pltpu.PrefetchScalarGridSpec(
            num_scalar_prefetch=1,
            grid=(channels // LANES,),
            in_specs=[
                pl.BlockSpec((LANES, 2, windows, samples), lambda c, p: (c, 0, 0, 0)),
                pl.BlockSpec((LANES, windows), lambda c, p: (c, 0)),
                pl.BlockSpec((2, samples, samples), lambda c, p: (0, 0, 0)),
            ],
            out_specs=pl.BlockSpec((half, 2 * windows, LANES), lambda c, p: (0, 0, c)),
            scratch_shapes=[
                pltpu.VMEM((half * (2 * windows + PAD), LANES), jnp.float32),
                pltpu.VMEM((windows, LANES), jnp.float32),
            ]
            + [pltpu.VMEM((LANES * (windows + PAD), LANES), jnp.float32)] * (samples // LANES),
        ),
        out_shape=jax.ShapeDtypeStruct((half, 2 * windows, channels), jnp.bfloat16),
        compiler_params=pltpu.CompilerParams(vmem_limit_bytes=32 * 2**20),
        name="whiten",
    )(pick, raw, clip, jnp.asarray(spectrum_tables(samples)))


def pairs_kernel(slots_ref, here_ref, *refs, pairs, nr, routes, nk, turn):
    rows, cols = refs[:nr], []
    at = nr
    for route in routes:
        cols.append(list(zip(refs[at : at + len(route)], route, strict=True)))
        at += len(route)
    t_ref = refs[at]
    out_ref, even_ref, odd_ref, a_ref, b_ref, o_ref, a_sem, b_sem, o_sem, tail_sem = refs[-10:]
    g = pl.program_id(0)
    last = len(pairs)
    half = a_ref.shape[1]
    windows = a_ref.shape[2] // 2
    chans = o_ref.shape[1]
    pitch = 2 * half + PAD
    rounds = half // nk
    ni = chans // rounds

    def row_copy(step):
        slot = step % 2
        return pltpu.make_async_copy(rows[pairs[step][0]], a_ref.at[slot], a_sem.at[slot])

    def col_copy(step, ref):
        slot = step % 2
        return pltpu.make_async_copy(ref, b_ref.at[slot], b_sem.at[slot])

    def start(step):
        row_copy(step).start()
        for ref, ways in cols[pairs[step][1]]:
            here = functools.reduce(jnp.logical_or, [here_ref[3] == way for way in ways])
            pl.when(here)(lambda: col_copy(step, ref).start())

    pl.when(g == 0)(lambda: start(0))
    for step in range(last):

        @pl.when(g == step)
        def _():
            if step + 1 < last:
                start(step + 1)
            row_copy(step).wait()
            col_copy(step, cols[pairs[step][1]][0][0]).wait()

    def cross(x_ref, it, slot):
        for u in range(nk):
            k = it * nk + u
            a = a_ref[slot, k]
            b = b_ref[slot, k]
            turned = jnp.concatenate([-b[windows:], b[:windows]], axis=0)
            both = jnp.concatenate([b, turned], axis=1)
            y = lax.dot_general(
                a, both, (((0,), (0,)), ((), ())), preferred_element_type=jnp.float32
            )
            x_ref[pl.ds(k, chans, stride=pitch), :] = y[:, :LANES]
            x_ref[pl.ds(half + k, chans, stride=pitch), :] = y[:, LANES:]

    def slab(x_ref, i):
        start = pl.multiple_of(i * pitch, 8)
        return x_ref[pl.ds(start, 2 * half), :].astype(jnp.bfloat16)

    def lag(x_ref, o, first, count):
        for u in range(0, count, 2):
            i = first + u
            x = jnp.concatenate([slab(x_ref, i), slab(x_ref, i + 1)], axis=1)
            y = jnp.dot(t_ref[...], x, preferred_element_type=jnp.float32).astype(jnp.bfloat16)
            o[i] = y[:, :LANES].T
            o[i + 1] = y[:, LANES:].T

    def loop(count, body):
        lax.fori_loop(0, count, lambda it, carry: (body(it), carry)[1], 0)

    back = jnp.maximum(g - 1, 0)
    block_r, block_c = block_at(back, slots_ref, here_ref, turn)
    same = here_ref[0] * turn[0] + block_r == here_ref[1] * turn[1] + block_c
    at_r, at_c = pl.multiple_of(block_r * LANES, LANES), pl.multiple_of(block_c * LANES, LANES)

    def write(slot, first, count, sem):
        return pltpu.make_async_copy(
            o_ref.at[slot, pl.ds(first, count)],
            out_ref.at[pl.ds(at_r + first, count), pl.ds(at_c, LANES), :],
            sem,
        )

    def clear(o, first, count):
        def one(u, carry):
            i = first + u
            start = pl.multiple_of(i // 16 * 16, 16)
            rows = o[i, pl.ds(start, 16), :]
            ids = lax.broadcasted_iota(jnp.int32, rows.shape, 0) + start
            kept = jnp.where(ids == i, 0.0, rows.astype(jnp.float32))
            o[i, pl.ds(start, 16), :] = kept.astype(jnp.bfloat16)
            return carry

        @pl.when(same)
        def _():
            lax.fori_loop(0, count, one, 0, unroll=8)

    def middle(new_ref, old_ref, slot):
        done = 1 - slot
        o = o_ref.at[done]
        pl.when(g >= 3)(lambda: write(done, 0, chans, o_sem.at[done]).wait())

        def body(it):
            cross(new_ref, it, slot)
            lag(old_ref, o, it * ni, ni)

        loop(rounds, body)
        clear(o, 0, chans)
        write(done, 0, chans, o_sem.at[done]).start()

    pl.when(g == 0)(lambda: loop(rounds, lambda it: cross(even_ref, it, 0)))
    if last > 1:
        pl.when((g > 0) & (g < last) & (g % 2 == 1))(lambda: middle(odd_ref, even_ref, 1))
    if last > 2:
        pl.when((g > 0) & (g < last) & (g % 2 == 0))(lambda: middle(even_ref, odd_ref, 0))

    @pl.when(g == last)
    def _():
        slot = (last - 1) % 2
        o = o_ref.at[slot]
        if last >= 3:
            write(slot, 0, chans, o_sem.at[slot]).wait()
        part = chans // TAIL

        def body(q):
            first = pl.multiple_of(q * part, part)
            lag(odd_ref if slot else even_ref, o, first, part)
            clear(o, first, part)
            write(slot, first, part, tail_sem.at[q]).start()

        loop(TAIL, body)
        if last >= 2:
            write(1 - slot, 0, chans, o_sem.at[1 - slot]).wait()
        for q in range(TAIL):
            write(slot, q * part, part, tail_sem.at[q]).wait()


def block_at(step, slots_ref, here_ref, turn):
    block_r = lax.rem(slots_ref[2 * step] + here_ref[2], turn[0])
    block_c = lax.rem(slots_ref[2 * step + 1] + here_ref[2], turn[1])
    return block_r, block_c


def correlate(rows, cols, pairs, table, here, shape, out):
    half, parts = rows[0].shape[:2]
    turn = (shape[0] // LANES, shape[1] // LANES)
    slots = jnp.asarray(np.array(pairs, np.int32).reshape(-1))

    used_r, used_c = sorted({r for r, _ in pairs}), sorted({c for _, c in pairs})
    pairs = [(used_r.index(r), used_c.index(c)) for r, c in pairs]
    whole = pl.BlockSpec(memory_space=pl.ANY)
    inputs = [rows[r] for r in used_r] + [v for c in used_c for v, _ in cols[c]]
    routes = [[ways for _, ways in cols[c]] for c in used_c]
    in_specs = [whole] * len(inputs) + [pl.BlockSpec(table.shape, lambda g, p, q: (0, 0))]
    inputs.append(table)
    aliases = {}
    if out is not None:
        aliases = {len(inputs) + 2: 0}
        inputs.append(out)
        in_specs.append(whole)
    steps = len(pairs)
    buffer = pltpu.VMEM((2, half, parts, LANES), jnp.bfloat16)
    return pl.pallas_call(
        functools.partial(
            pairs_kernel, pairs=pairs, nr=len(used_r), routes=routes, nk=half // 2, turn=turn
        ),
        grid_spec=pltpu.PrefetchScalarGridSpec(
            num_scalar_prefetch=2,
            grid=(steps + 1,),
            in_specs=in_specs,
            out_specs=whole,
            scratch_shapes=[pltpu.VMEM((LANES * (2 * half + PAD), LANES), jnp.float32)] * 2
            + [buffer, buffer, pltpu.VMEM((2, LANES, LANES, shape[2]), jnp.bfloat16)]
            + [pltpu.SemaphoreType.DMA((2,))] * 3
            + [pltpu.SemaphoreType.DMA((TAIL,))],
        ),
        out_shape=jax.ShapeDtypeStruct(shape, jnp.bfloat16),
        input_output_aliases=aliases,
        compiler_params=pltpu.CompilerParams(vmem_limit_bytes=56 * 2**20),
        cost_estimate=pl.CostEstimate(
            flops=int((7 * steps + 5) * 1e9), bytes_accessed=steps * 2**22, transcendentals=0
        ),
        name="pairs",
    )(slots, here, *inputs)


def hop(v, bit, held, n_col):
    moves = [(r * n_col + c, (r ^ bit) * n_col + c) for c in range(n_col) for r in sorted(held[c])]
    for kept in held:
        kept |= {r ^ bit for r in kept}
    return lax.ppermute(v, ("row", "col"), moves)


def send(v, n_row, n_col):
    return [
        lax.ppermute(v, ("row", "col"), [(c * n_col + c, (c ^ d) * n_col + c) for c in range(n_col)])
        for d in range(1, n_row)
    ]


def gate(v, after):
    return lax.optimization_barrier((v, after))[0]


def local(raw_traces, channel_pick, clip_mask, *, n_row, n_col):
    owned = channel_pick.shape[0]
    windows = raw_traces.shape[1]
    samples = raw_traces.shape[2]
    half = samples // 2
    row, col = lax.axis_index("row"), lax.axis_index("col")
    raw = raw_traces.reshape(owned, 2, windows, samples)
    table = jnp.asarray(lag_table(samples, L, windows))
    tile_r, tile_c = owned * n_col, owned * n_row
    shape = (tile_r, tile_c, L)

    if owned != LANES or n_row != n_col or n_row & (n_row - 1) or n_row < 4:
        fill = -owned % LANES
        raw = jnp.pad(raw, ((0, fill), (0, 0), (0, 0), (0, 0)))
        pick, clip = jnp.pad(channel_pick, (0, fill)), jnp.pad(clip_mask, ((0, fill), (0, 0)))
        z = whiten(raw, pick, clip)[:, :, :owned]
        first = lax.all_gather(z, "col", axis=2, tiled=True)
        second = lax.psum(jnp.where(row == col, first, 0).astype(first.dtype), "row")
        nr, nc = tile_r // LANES, tile_c // LANES
        rows = jnp.split(first, nr, axis=2)
        cols = [[(v, [0])] for v in jnp.split(second, nc, axis=2)]
        pairs = [(r, c) for r in range(nr) for c in range(nc)]
        return correlate(rows, cols, pairs, table, jnp.stack([row, col, 0 * col, 0 * col]), shape, None)

    n = n_col
    ring = [(j, (j - 1) % n) for j in range(n)]
    here = jnp.stack([row, col, col, row ^ col])

    def step(pairs, out):
        return correlate(rows, cols, pairs, table, here, shape, out)

    def spread(v, got, held):
        bit = n_row // 2
        while bit > 1:
            v = jnp.where(((row ^ col) & bit) == 0, v, got)
            bit //= 2
            got = hop(v, bit, held, n_col)
        return [(v, list(range(0, n_row, 2))), (got, list(range(1, n_row, 2)))]

    top = n_row // 2
    rows = [whiten(raw, channel_pick, clip_mask)]
    rows.append(lax.ppermute(rows[0], "col", ring))
    held = [{c} for c in range(n_col)]
    cols = [spread(rows[0], hop(rows[0], top, held, n_col), held)]
    out = None
    pairs = [(0, 0), (1, 0)]
    for s in range(2, n + 1):
        if s < n:
            rows.append(lax.ppermute(rows[s - 1], "col", ring))
        if s == 2:
            held = [{c} for c in range(n_col)]
            coming = [hop(rows[1], top, held, n_col)]
        else:
            coming = send(rows[s - 1], n_row, n_col)
        out = step(pairs, out)
        if s < n:
            rows[s] = gate(rows[s], out)
        coming = [gate(v, out) for v in coming]
        if s == 2:
            cols.append(spread(rows[1], coming[0], held))
        else:
            cols.append([(v, [d]) for d, v in enumerate([rows[s - 1], *coming])])
        pairs = [(r, s - 1) for r in range(min(s, n - 1) + 1)] + [(s, c) for c in range(s - 1) if s < n]
    return step(pairs, out)


def solution(mesh):
    return jax.shard_map(
        functools.partial(local, n_row=mesh.shape["row"], n_col=mesh.shape["col"]),
        mesh=mesh,
        in_specs=(
            P(("seg", "row", "col"), None, None),
            P(("seg", "row", "col")),
            P(("seg", "row", "col"), None),
        ),
        out_specs=P(("seg", "row"), "col", None),
        check_vma=False,
    )
```

```python
import functools
import math

import jax
import jax.numpy as jnp
import ml_dtypes
import numpy as np
from jax import lax
from jax.experimental import pallas as pl
from jax.experimental.pallas import tpu as pltpu
from jax.sharding import PartitionSpec as P

L = 128
LANES = 128
PAD = 8
TAIL = 4


def spectrum_tables(samples):
    half = samples // 2
    freq = np.arange(1, half + 1)
    pos = np.arange(samples)
    angle = (freq[:, None] * pos[None, :] % samples) * (2.0 * np.pi / samples)
    table = np.concatenate([np.cos(angle), -np.sin(angle)], axis=0).astype(np.float32)
    high = table.astype(ml_dtypes.bfloat16)
    low = (table - high.astype(np.float32)).astype(ml_dtypes.bfloat16)
    return np.stack([high, low])


def lag_table(samples, lags, windows):
    half = samples // 2
    freq = np.arange(1, half + 1)
    shift = np.arange(lags) - lags // 2
    angle = (freq[:, None] * shift[None, :] % samples) * (2.0 * np.pi / samples)
    scale = 1.0 / math.sqrt(windows * half)
    table = np.concatenate([np.cos(angle), -np.sin(angle)], axis=0) * scale
    return table.T.astype(ml_dtypes.bfloat16)


def whiten_kernel(pick_ref, raw_ref, clip_ref, table_ref, z_ref, rows_ref, *picked):
    windows = raw_ref.shape[2]
    gap = windows + PAD
    first = pl.program_id(0) * LANES
    half = table_ref.shape[1] // 2
    parts = 2 * windows
    pitch = parts + PAD
    contract = (((1,), (1,)), ((), ()))

    def pull(j, carry):
        record = raw_ref[j, lax.rem(pick_ref[first + j], 2)].astype(jnp.float32)
        start = pl.multiple_of(j * gap, 8)
        for q, part in enumerate(picked):
            part[pl.ds(start, windows), :] = record[:, q * LANES : (q + 1) * LANES]
        return carry

    lax.fori_loop(0, LANES, pull, 0, unroll=8)

    def window(w, carry):
        raw = jnp.concatenate([part[pl.ds(w, LANES, stride=gap), :] for part in picked], axis=1)
        raw = raw.astype(jnp.bfloat16)
        spec = lax.dot_general(table_ref[0], raw, contract, preferred_element_type=jnp.float32)
        spec += lax.dot_general(table_ref[1], raw, contract, preferred_element_type=jnp.float32)
        real, imag = spec[:half], spec[half:]
        power = real * real + imag * imag
        total = power
        for far in (1, 2):
            edge = jnp.zeros((far, power.shape[1]), jnp.float32)
            total += jnp.concatenate([power[far:], edge], axis=0)
            total += jnp.concatenate([edge, power[:-far]], axis=0)
        mean = jnp.sum(power, axis=0, keepdims=True) * (1.0 / half)
        denom = jnp.sqrt(total * 0.2 + 0.1 * mean + 1e-06)
        weight = clip_ref[pl.ds(w, 1), :].astype(jnp.float32) / denom
        rows_ref[pl.ds(w, half, stride=pitch), :] = real * weight
        rows_ref[pl.ds(windows + w, half, stride=pitch), :] = imag * weight
        return carry

    lax.fori_loop(0, windows, window, 0, unroll=4)

    def narrow(k, carry):
        start = pl.multiple_of(k * pitch, 8)
        z_ref[k] = rows_ref[pl.ds(start, parts), :].astype(jnp.bfloat16)
        return carry

    lax.fori_loop(0, half, narrow, 0, unroll=8)


def whiten(raw, pick, clip):
    channels, _, windows, samples = raw.shape
    half = samples // 2
    return pl.pallas_call(
        whiten_kernel,
        grid_spec=pltpu.PrefetchScalarGridSpec(
            num_scalar_prefetch=1,
            grid=(channels // LANES,),
            in_specs=[
                pl.BlockSpec((LANES, 2, windows, samples), lambda c, p: (c, 0, 0, 0)),
                pl.BlockSpec((windows, LANES), lambda c, p: (0, c)),
                pl.BlockSpec((2, samples, samples), lambda c, p: (0, 0, 0)),
            ],
            out_specs=pl.BlockSpec((half, 2 * windows, LANES), lambda c, p: (0, 0, c)),
            scratch_shapes=[
                pltpu.VMEM((half * (2 * windows + PAD), LANES), jnp.float32),
            ]
            + [pltpu.VMEM((LANES * (windows + PAD), LANES), jnp.float32)] * (samples // LANES),
        ),
        out_shape=jax.ShapeDtypeStruct((half, 2 * windows, channels), jnp.bfloat16),
        compiler_params=pltpu.CompilerParams(vmem_limit_bytes=32 * 2**20),
        name="whiten",
    )(pick, raw, clip, jnp.asarray(spectrum_tables(samples)))


def pairs_kernel(slots_ref, here_ref, *refs, pairs, nr, routes, nk, turn):
    rows, cols = refs[:nr], []
    at = nr
    for route in routes:
        cols.append(list(zip(refs[at : at + len(route)], route, strict=True)))
        at += len(route)
    t_ref = refs[at]
    out_ref, even_ref, odd_ref, a_ref, b_ref, o_ref, a_sem, b_sem, o_sem, tail_sem = refs[-10:]
    g = pl.program_id(0)
    last = len(pairs)
    half = a_ref.shape[1]
    windows = a_ref.shape[2] // 2
    chans = o_ref.shape[1]
    pitch = 2 * half + PAD
    rounds = half // nk
    ni = chans // rounds

    def row_copy(step):
        slot = step % 2
        return pltpu.make_async_copy(rows[pairs[step][0]], a_ref.at[slot], a_sem.at[slot])

    def col_copy(step, ref):
        slot = step % 2
        return pltpu.make_async_copy(ref, b_ref.at[slot], b_sem.at[slot])

    def start(step):
        row_copy(step).start()
        for ref, ways in cols[pairs[step][1]]:
            here = functools.reduce(jnp.logical_or, [here_ref[3] == way for way in ways])
            pl.when(here)(lambda: col_copy(step, ref).start())

    pl.when(g == 0)(lambda: start(0))
    for step in range(last):

        @pl.when(g == step)
        def _():
            if step + 1 < last:
                start(step + 1)
            row_copy(step).wait()
            col_copy(step, cols[pairs[step][1]][0][0]).wait()

    def cross(x_ref, it, slot):
        for u in range(nk):
            k = it * nk + u
            a = a_ref[slot, k]
            b = b_ref[slot, k]
            turned = jnp.concatenate([-b[windows:], b[:windows]], axis=0)
            both = jnp.concatenate([b, turned], axis=1)
            y = lax.dot_general(
                a, both, (((0,), (0,)), ((), ())), preferred_element_type=jnp.float32
            )
            x_ref[pl.ds(k, chans, stride=pitch), :] = y[:, :LANES]
            x_ref[pl.ds(half + k, chans, stride=pitch), :] = y[:, LANES:]

    def slab(x_ref, i):
        start = pl.multiple_of(i * pitch, 8)
        return x_ref[pl.ds(start, 2 * half), :].astype(jnp.bfloat16)

    def lag(x_ref, o, first, count):
        for u in range(0, count, 2):
            i = first + u
            x = jnp.concatenate([slab(x_ref, i), slab(x_ref, i + 1)], axis=1)
            y = jnp.dot(t_ref[...], x, preferred_element_type=jnp.float32).astype(jnp.bfloat16)
            o[i] = y[:, :LANES].T
            o[i + 1] = y[:, LANES:].T

    def loop(count, body):
        lax.fori_loop(0, count, lambda it, carry: (body(it), carry)[1], 0)

    back = jnp.maximum(g - 1, 0)
    block_r, block_c = block_at(back, slots_ref, here_ref, turn)
    same = here_ref[0] * turn[0] + block_r == here_ref[1] * turn[1] + block_c
    at_r, at_c = pl.multiple_of(block_r * LANES, LANES), pl.multiple_of(block_c * LANES, LANES)

    def write(slot, first, count, sem):
        return pltpu.make_async_copy(
            o_ref.at[slot, pl.ds(first, count)],
            out_ref.at[pl.ds(at_r + first, count), pl.ds(at_c, LANES), :],
            sem,
        )

    def clear(o, first, count):
        def one(u, carry):
            i = first + u
            start = pl.multiple_of(i // 16 * 16, 16)
            rows = o[i, pl.ds(start, 16), :]
            ids = lax.broadcasted_iota(jnp.int32, rows.shape, 0) + start
            kept = jnp.where(ids == i, 0.0, rows.astype(jnp.float32))
            o[i, pl.ds(start, 16), :] = kept.astype(jnp.bfloat16)
            return carry

        @pl.when(same)
        def _():
            lax.fori_loop(0, count, one, 0, unroll=8)

    def middle(new_ref, old_ref, slot):
        done = 1 - slot
        o = o_ref.at[done]
        pl.when(g >= 3)(lambda: write(done, 0, chans, o_sem.at[done]).wait())

        def body(it):
            cross(new_ref, it, slot)
            lag(old_ref, o, it * ni, ni)

        loop(rounds, body)
        clear(o, 0, chans)
        write(done, 0, chans, o_sem.at[done]).start()

    pl.when(g == 0)(lambda: loop(rounds, lambda it: cross(even_ref, it, 0)))
    if last > 1:
        pl.when((g > 0) & (g < last) & (g % 2 == 1))(lambda: middle(odd_ref, even_ref, 1))
    if last > 2:
        pl.when((g > 0) & (g < last) & (g % 2 == 0))(lambda: middle(even_ref, odd_ref, 0))

    @pl.when(g == last)
    def _():
        slot = (last - 1) % 2
        o = o_ref.at[slot]
        if last >= 3:
            write(slot, 0, chans, o_sem.at[slot]).wait()
        part = chans // TAIL

        def body(q):
            first = pl.multiple_of(q * part, part)
            lag(odd_ref if slot else even_ref, o, first, part)
            clear(o, first, part)
            write(slot, first, part, tail_sem.at[q]).start()

        loop(TAIL, body)
        if last >= 2:
            write(1 - slot, 0, chans, o_sem.at[1 - slot]).wait()
        for q in range(TAIL):
            write(slot, q * part, part, tail_sem.at[q]).wait()


def block_at(step, slots_ref, here_ref, turn):
    block_r = lax.rem(slots_ref[2 * step] + here_ref[2], turn[0])
    block_c = lax.rem(slots_ref[2 * step + 1] + here_ref[2], turn[1])
    return block_r, block_c


def correlate(rows, cols, pairs, table, here, shape, out):
    half, parts = rows[0].shape[:2]
    turn = (shape[0] // LANES, shape[1] // LANES)
    slots = jnp.asarray(np.array(pairs, np.int32).reshape(-1))

    used_r, used_c = sorted({r for r, _ in pairs}), sorted({c for _, c in pairs})
    pairs = [(used_r.index(r), used_c.index(c)) for r, c in pairs]
    whole = pl.BlockSpec(memory_space=pl.ANY)
    inputs = [rows[r] for r in used_r] + [v for c in used_c for v, _ in cols[c]]
    routes = [[ways for _, ways in cols[c]] for c in used_c]
    in_specs = [whole] * len(inputs) + [pl.BlockSpec(table.shape, lambda g, p, q: (0, 0))]
    inputs.append(table)
    aliases = {}
    if out is not None:
        aliases = {len(inputs) + 2: 0}
        inputs.append(out)
        in_specs.append(whole)
    steps = len(pairs)
    buffer = pltpu.VMEM((2, half, parts, LANES), jnp.bfloat16)
    return pl.pallas_call(
        functools.partial(
            pairs_kernel, pairs=pairs, nr=len(used_r), routes=routes, nk=half // 2, turn=turn
        ),
        grid_spec=pltpu.PrefetchScalarGridSpec(
            num_scalar_prefetch=2,
            grid=(steps + 1,),
            in_specs=in_specs,
            out_specs=whole,
            scratch_shapes=[pltpu.VMEM((LANES * (2 * half + PAD), LANES), jnp.float32)] * 2
            + [buffer, buffer, pltpu.VMEM((2, LANES, LANES, shape[2]), jnp.bfloat16)]
            + [pltpu.SemaphoreType.DMA((2,))] * 3
            + [pltpu.SemaphoreType.DMA((TAIL,))],
        ),
        out_shape=jax.ShapeDtypeStruct(shape, jnp.bfloat16),
        input_output_aliases=aliases,
        compiler_params=pltpu.CompilerParams(vmem_limit_bytes=56 * 2**20),
        cost_estimate=pl.CostEstimate(
            flops=int((7 * steps + 5) * 1e9), bytes_accessed=steps * 2**22, transcendentals=0
        ),
        name="pairs",
    )(slots, here, *inputs)


def hop(v, bit, held, n_col):
    moves = [(r * n_col + c, (r ^ bit) * n_col + c) for c in range(n_col) for r in sorted(held[c])]
    for kept in held:
        kept |= {r ^ bit for r in kept}
    return lax.ppermute(v, ("row", "col"), moves)


def send(v, n_row, n_col):
    return [
        lax.ppermute(v, ("row", "col"), [(c * n_col + c, (c ^ d) * n_col + c) for c in range(n_col)])
        for d in range(1, n_row)
    ]


def gate(v, after):
    return lax.optimization_barrier((v, after))[0]


def local(raw_traces, channel_pick, clip_mask, *, n_row, n_col):
    owned = channel_pick.shape[0]
    windows = raw_traces.shape[1]
    samples = raw_traces.shape[2]
    half = samples // 2
    row, col = lax.axis_index("row"), lax.axis_index("col")
    raw = raw_traces.reshape(owned, 2, windows, samples)
    clip = clip_mask.T
    table = jnp.asarray(lag_table(samples, L, windows))
    tile_r, tile_c = owned * n_col, owned * n_row
    shape = (tile_r, tile_c, L)

    if owned != LANES or n_row != n_col or n_row & (n_row - 1) or n_row < 4:
        fill = -owned % LANES
        raw = jnp.pad(raw, ((0, fill), (0, 0), (0, 0), (0, 0)))
        pick, clip = jnp.pad(channel_pick, (0, fill)), jnp.pad(clip, ((0, 0), (0, fill)))
        z = whiten(raw, pick, clip)[:, :, :owned]
        first = lax.all_gather(z, "col", axis=2, tiled=True)
        second = lax.psum(jnp.where(row == col, first, 0).astype(first.dtype), "row")
        nr, nc = tile_r // LANES, tile_c // LANES
        rows = jnp.split(first, nr, axis=2)
        cols = [[(v, [0])] for v in jnp.split(second, nc, axis=2)]
        pairs = [(r, c) for r in range(nr) for c in range(nc)]
        return correlate(rows, cols, pairs, table, jnp.stack([row, col, 0 * col, 0 * col]), shape, None)

    n = n_col
    ring = [(j, (j - 1) % n) for j in range(n)]
    here = jnp.stack([row, col, col, row ^ col])

    def step(pairs, out):
        return correlate(rows, cols, pairs, table, here, shape, out)

    def spread(v, got, held):
        bit = n_row // 2
        while bit > 1:
            v = jnp.where(((row ^ col) & bit) == 0, v, got)
            bit //= 2
            got = hop(v, bit, held, n_col)
        return [(v, list(range(0, n_row, 2))), (got, list(range(1, n_row, 2)))]

    top = n_row // 2
    rows = [whiten(raw, channel_pick, clip)]
    rows.append(lax.ppermute(rows[0], "col", ring))
    held = [{c} for c in range(n_col)]
    cols = [spread(rows[0], hop(rows[0], top, held, n_col), held)]
    out = None
    pairs = [(0, 0), (1, 0)]
    for s in range(2, n + 1):
        if s < n:
            rows.append(lax.ppermute(rows[s - 1], "col", ring))
        if s == 2:
            held = [{c} for c in range(n_col)]
            coming = [hop(rows[1], top, held, n_col)]
        else:
            coming = send(rows[s - 1], n_row, n_col)
        out = step(pairs, out)
        if s < n:
            rows[s] = gate(rows[s], out)
        coming = [gate(v, out) for v in coming]
        if s == 2:
            cols.append(spread(rows[1], coming[0], held))
        else:
            cols.append([(v, [d]) for d, v in enumerate([rows[s - 1], *coming])])
        pairs = [(r, s - 1) for r in range(min(s, n - 1) + 1)] + [(s, c) for c in range(s - 1) if s < n]
    return step(pairs, out)


def solution(mesh):
    return jax.shard_map(
        functools.partial(local, n_row=mesh.shape["row"], n_col=mesh.shape["col"]),
        mesh=mesh,
        in_specs=(
            P(("seg", "row", "col"), None, None),
            P(("seg", "row", "col")),
            P(("seg", "row", "col"), None),
        ),
        out_specs=P(("seg", "row"), "col", None),
        check_vma=False,
    )
```
